32 devices in a mesh: band: 32 (over z, y, x, core).
Axes of the slice: x: 2, y: 2, z: 4, core: 2. Of those that a mesh axis runs over, the one named last changes fastest.
Arguments:
- orbitals: float32 [32, 64, 4096], P('band'), may hold values from -6 to 6
- kernel_values: float32 [32], replicated, may hold values from 0.2 to 4
- shell_index: int32 [64, 4096], replicated, may hold values from 0 to 31, as said below
Outputs:
- exchange_term: float32 [32, 64, 4096], P('band')
- margin: float32 [32, 32], P('band')
The draws below stay inside these ranges and needn't reach their ends.
Inputs may be any that keep to these rules, and one draw needn't show every extreme that they name: `shell_index`: the class of a wave vector is unchanged when any one of its indices a is replaced by (64 - a) mod 64.
All inputs are finite; a program needn't handle non-finite values.
Results may differ from the reference program's by a relative error of at most 0.0003.
Values sent between devices are 32-bit elements; how exact they have to be, the bound alone decides.
No kernel may reach another device: no remote copies, remote signals or barrier semaphores. Data moves between devices by JAX's collectives and lax.ppermute only.
A program may use at most 64 MiB of HBM per device.

```python
import math
import jax
import jax.numpy as jnp
from jax import lax

GRID = 64
NSHELL = 32
NBD = 1
STEPS = 2
BANDS = 32
N_BAND = 32


def draw_shell_index(key, part):
    half_count = GRID // 2 + 1
    classes = jax.random.randint(key, (half_count, half_count, half_count), 0, NSHELL)
    positions = jnp.arange(GRID, dtype=jnp.int32)
    mirrored = jnp.minimum(positions, GRID - positions)
    whole_grid = classes[mirrored][:, mirrored][:, :, mirrored]
    return whole_grid.reshape(GRID, GRID * GRID).astype(jnp.int32)


def block_levels(rng, dims, shards, smallest, largest):
    loudness = 1.0
    for axis_at, parts in shards:
        draws = jax.random.uniform(jax.random.fold_in(jax.random.fold_in(rng, 6), axis_at), (parts,), jnp.float32, smallest / len(shards), largest / len(shards))
        loudness = loudness * jnp.repeat(jnp.exp(draws), dims[axis_at] // parts).reshape((-1,) + (1,) * (len(dims) - 1 - axis_at))
    return loudness


def normal_values(key, shape, spread, reach, cuts=(), kind=jnp.bfloat16):
    result = jax.random.normal(key, shape, jnp.float32) * spread
    if len(cuts) > 0:
        result = block_levels(key, shape, cuts, -0.22, 0.18) * result
    return jnp.clip(result, min=-reach, max=reach).astype(kind)


def setup_inputs(seed: int = 0) -> dict:
    keys = jax.random.split(jax.random.key(seed), 4)
    orbitals = normal_values(keys[0], (BANDS, GRID, GRID * GRID), 1.0, 6.0, ((0, 32),), jnp.float32)
    kernel_values = jnp.clip(jnp.exp(jax.random.uniform(keys[1], (NSHELL,), jnp.float32, math.log(0.2), math.log(4.0))), 0.2, 4.0)
    shell_index = draw_shell_index(jax.random.fold_in(keys[3], 71), 0)
    return dict(orbitals=orbitals, kernel_values=kernel_values, shell_index=shell_index)


def reference(orbitals, kernel_values, shell_index):
    volume = GRID ** 3
    kernel = kernel_values[shell_index].reshape(GRID, GRID, GRID)[:, :, : GRID // 2 + 1]
    orbital_cubes = orbitals.reshape(BANDS, GRID, GRID, GRID)

    def block_term(block_index):
        shifts = jnp.arange(-STEPS, STEPS + 1, dtype=jnp.int32)
        partner_blocks = (block_index + shifts) % N_BAND
        band_rows = (partner_blocks[:, None] * NBD + jnp.arange(NBD, dtype=jnp.int32)[None]).reshape(-1)
        partners = jnp.take(orbital_cubes, band_rows, axis=0)
        own_bands = lax.dynamic_slice_in_dim(orbital_cubes, (block_index * NBD).astype(jnp.int32), NBD, 0)

        def one_orbital(single):
            density = single[None] * partners
            spectrum = jnp.fft.rfftn(density, axes=(1, 2, 3)) * kernel[None]
            potential = jnp.fft.irfftn(spectrum, s=(GRID, GRID, GRID), axes=(1, 2, 3))
            return -jnp.sum(potential * partners, axis=0)

        return lax.map(one_orbital, own_bands)

    exchange_terms = lax.map(block_term, jnp.arange(N_BAND, dtype=jnp.int32))
    exchange_terms = exchange_terms.reshape(BANDS, GRID, GRID * GRID)
    margin = jnp.dot(orbitals.reshape(BANDS, volume), exchange_terms.reshape(BANDS, volume).T,
                      precision=lax.Precision.HIGHEST, preferred_element_type=jnp.float32) / volume
    return exchange_terms, margin
```

```python
import functools

import jax
import jax.numpy as jnp
import ml_dtypes
import numpy as np
from jax import lax
from jax.experimental import pallas as pl
from jax.experimental.pallas import tpu as pltpu
from jax.sharding import PartitionSpec as P

CHUNKS = 2
LANES = 128
SUBLANES = 8
f32, bf16 = jnp.float32, jnp.bfloat16
VMEM = pl.BlockSpec(memory_space=pltpu.VMEM)


def tables(g):
    index = np.arange(g)
    angle = 2.0 * np.pi / g * (np.outer(index, index) % g)
    cas = np.cos(angle) + np.sin(angle)
    hi = cas.astype(np.float32).astype(ml_dtypes.bfloat16)
    lo = (cas - hi.astype(np.float64)).astype(np.float32).astype(ml_dtypes.bfloat16)
    rows = np.concatenate([hi, hi, lo], axis=1)
    eye = np.eye(LANES // g, dtype=np.float32)
    wide_hi = np.kron(eye, hi.astype(np.float32)).astype(ml_dtypes.bfloat16)
    wide_lo = np.kron(eye, lo.astype(np.float32)).astype(ml_dtypes.bfloat16)
    lanes = np.block([[wide_hi, wide_lo], [wide_hi, np.zeros_like(wide_lo)]])
    return jnp.asarray(rows), jnp.asarray(lanes)


def split(value):
    hi = value.astype(bf16)
    lo = (value - hi.astype(f32)).astype(bf16)
    return hi, lo


def rows_pass(table, value):
    hi, lo = split(value)
    stacked = jnp.concatenate([hi, lo, hi], axis=0)
    return jnp.dot(table, stacked, preferred_element_type=f32)


def lanes_pass(value, table):
    hi, lo = split(value)
    both = jnp.concatenate([hi, lo], axis=1)
    result = jnp.dot(both, table, preferred_element_type=f32)
    return result[:, :LANES] + result[:, LANES:]


def exchange_halves(value, g):
    half = g // 2
    low = lax.broadcasted_iota(jnp.int32, (half, LANES), 1) < g
    parts = []
    for start in range(0, value.shape[0], g):
        first = value[start : start + half]
        second = value[start + half : start + g]
        parts.append(jnp.where(low, first, pltpu.roll(second, g, 1)))
        parts.append(jnp.where(low, pltpu.roll(first, g, 1), second))
    return jnp.concatenate(parts, axis=0)


def pair_kernel(g, n_right, n_other, has_acc, tiled, *refs):
    refs = list(refs)
    left = refs.pop(0)
    right_refs = [refs.pop(0) for _ in range(n_right)]
    other_refs = [refs.pop(0) for _ in range(n_other)]
    flag = refs.pop(0) if n_other else None
    acc = refs.pop(0) if has_acc else None
    kern, rows_table, lanes_table = refs[:3]
    out = refs[3]
    tiles = refs[4] if tiled else None
    work = refs[-1]
    half = g // 2
    width = 2 * LANES
    table = rows_table[...]
    wide = lanes_table[...]

    def load(parts, cols):
        return jnp.concatenate([part[:, cols] for part in parts], axis=0)

    def right_block(cols):
        value = load(right_refs, cols)
        if n_other:
            value = jnp.where(flag[0] > 0, value, load(other_refs, cols))
        return value

    for step in range(g * g // width):
        cols = slice(step * width, (step + 1) * width)
        first = rows_pass(table, left[:, cols] * right_block(cols))
        first = jnp.concatenate([first[:, :LANES], first[:, LANES:]], axis=0)
        second = exchange_halves(lanes_pass(first, wide), g)
        work[step * 2 * g : (step + 1) * 2 * g, :] = second

    for step in range(half // 2):
        plane = 2 * step
        value = jnp.concatenate(
            [work[pl.ds(plane + k, g, stride=half), :] for k in range(2)], axis=1
        )
        scale = kern[plane * g : (plane + 2) * g, :]
        scale = jnp.concatenate([scale[:g], scale[g:]], axis=1)
        value = rows_pass(table, rows_pass(table, value) * scale)
        for k in range(2):
            work[pl.ds(plane + k, g, stride=half), :] = value[:, k * LANES : (k + 1) * LANES]

    for step in range(g * g // width):
        cols = slice(step * width, (step + 1) * width)
        value = exchange_halves(lanes_pass(work[step * 2 * g : (step + 1) * 2 * g, :], wide), g)
        value = rows_pass(table, jnp.concatenate([value[:g], value[g:]], axis=1))
        value = value * right_block(cols)
        if has_acc:
            value = acc[:, cols] + value
        out[:, cols] = value
        if tiled:
            tiles[2 * step * g : (2 * step + 1) * g, :] = value[:, :LANES]
            tiles[(2 * step + 1) * g : (2 * step + 2) * g, :] = value[:, LANES:]


def pair(left, right, acc, kern, consts, other=(), flag=None, tiled=False):
    g = left.shape[0]
    operands = [left, *right, *other]
    specs = [VMEM] * len(operands)
    if other:
        operands.append(flag)
        specs.append(pl.BlockSpec(memory_space=pltpu.SMEM))
    if acc is not None:
        operands.append(acc)
        specs.append(VMEM)
    operands += [kern, *consts]
    specs += [VMEM] * 3
    shapes = [jax.ShapeDtypeStruct(left.shape, f32)]
    if tiled:
        shapes.append(jax.ShapeDtypeStruct((g * g * g // LANES, LANES), f32))
    points = g**3
    result = pl.pallas_call(
        functools.partial(pair_kernel, g, len(right), len(other), acc is not None, tiled),
        out_shape=shapes,
        in_specs=specs,
        out_specs=[VMEM] * len(shapes),
        scratch_shapes=[pltpu.VMEM((points // LANES, LANES), f32)],
        compiler_params=pltpu.CompilerParams(vmem_limit_bytes=32 * 2**20),
        cost_estimate=pl.CostEstimate(
            flops=12 * points * LANES * 6, bytes_accessed=16 * points, transcendentals=0
        ),
    )(*operands)
    return result if tiled else result[0]


def lookup_kernel(scale, values, index, out):
    rows = values[...]
    size = index.shape[0] // 16
    for step in range(16):
        part = index[step * size : (step + 1) * size, :]
        table = jnp.broadcast_to(rows, part.shape)
        out[step * size : (step + 1) * size, :] = jnp.take_along_axis(table, part, axis=1) * scale


def lookup(kernel_values, shell_index):
    g = shell_index.shape[0]
    classes = kernel_values.shape[0]
    index = shell_index.reshape(2, g // 2, g, g).transpose(1, 2, 0, 3).reshape(-1, LANES)
    padded = jnp.pad(kernel_values, (0, LANES - classes)).reshape(1, LANES)
    return pl.pallas_call(
        functools.partial(lookup_kernel, -1.0 / g**3),
        out_shape=jax.ShapeDtypeStruct(index.shape, f32),
        in_specs=[VMEM] * 2,
        out_specs=VMEM,
    )(padded, index)


def margin_kernel(scale, orbitals, terms, out):
    count = orbitals.shape[0]
    lefts, rights = [], []
    for step in range(orbitals.shape[1] // SUBLANES):
        rows = slice(step * SUBLANES, (step + 1) * SUBLANES)
        a_hi, a_lo = split(orbitals[:, rows, :].reshape(count * SUBLANES, LANES))
        b_hi, b_lo = split(terms[:, rows, :].reshape(count * SUBLANES, LANES))
        lefts += [a_hi, a_lo, a_hi]
        rights += [b_hi, b_hi, b_lo]
    products = lax.dot_general(
        jnp.concatenate(lefts, axis=1),
        jnp.concatenate(rights, axis=1),
        (((1,), (1,)), ((), ())),
        preferred_element_type=f32,
    )
    size = count * SUBLANES
    row = lax.broadcasted_iota(jnp.int32, (size, size), 0) % SUBLANES
    col = lax.broadcasted_iota(jnp.int32, (size, size), 1) % SUBLANES
    kept = jnp.where(row == col, products, 0.0)
    summed = jnp.sum(kept.reshape(count, SUBLANES, size), axis=1)
    pick_row = lax.broadcasted_iota(jnp.int32, (size, count), 0) // SUBLANES
    pick_col = lax.broadcasted_iota(jnp.int32, (size, count), 1)
    pick = (pick_row == pick_col).astype(f32)
    out[...] = scale * jnp.dot(
        summed, pick, precision=lax.Precision.HIGHEST, preferred_element_type=f32
    )


def partial_margin(orbitals, terms, points):
    count = orbitals.shape[0]
    return pl.pallas_call(
        functools.partial(margin_kernel, 1.0 / points),
        out_shape=jax.ShapeDtypeStruct((count, count), f32),
        in_specs=[VMEM] * 2,
        out_specs=VMEM,
        compiler_params=pltpu.CompilerParams(vmem_limit_bytes=48 * 2**20),
    )(orbitals, terms)


def permute(value, target, count):
    return lax.ppermute(value, "band", [(source, target(source) % count) for source in range(count)])


def far_target(source):
    return source - 4 if (source // 2) % 2 else source + 4


def local(orbitals, kernel_values, shell_index):
    count = lax.axis_size("band")
    me = lax.axis_index("band")
    g = shell_index.shape[0]
    points = g**3
    consts = tables(g)
    own = orbitals.reshape(g, g * g)

    size = g // CHUNKS
    near = [permute(own[k * size : (k + 1) * size], lambda d: d ^ 2, count) for k in range(CHUNKS)]
    peer = permute(own, lambda d: d ^ 1, count)
    far = [permute(part, far_target, count) for part in near]
    near_cross = [permute(part, lambda d: d ^ 1, count) for part in near]
    far_cross = [permute(part, lambda d: d ^ 1, count) for part in far]
    use_near = (((me + 1) // 2) % 2).astype(jnp.int32).reshape(1)

    kern = lookup(kernel_values, shell_index)
    by_tile = own.reshape(g, g * g // LANES, LANES).transpose(1, 0, 2).reshape(count, -1, LANES)
    spread_orbitals = lax.all_to_all(by_tile, "band", split_axis=0, concat_axis=0, tiled=True)

    term = pair(own, [own], None, kern, consts)
    term = pair(own, [peer], term, kern, consts)
    term = pair(own, near, term, kern, consts)
    term = pair(own, far, term, kern, consts)
    term, tiles = pair(own, near_cross, term, kern, consts, far_cross, use_near, tiled=True)

    spread_terms = lax.all_to_all(
        tiles.reshape(count, -1, LANES), "band", split_axis=0, concat_axis=0, tiled=True
    )
    rows = partial_margin(spread_orbitals, spread_terms, points)
    rows = lax.all_to_all(rows, "band", split_axis=0, concat_axis=0, tiled=True)
    margin = jnp.sum(rows, axis=0, keepdims=True)
    return term.reshape(orbitals.shape), margin


def solution(mesh):
    return jax.shard_map(
        local,
        mesh=mesh,
        in_specs=(P("band", None, None), P(), P()),
        out_specs=(P("band", None, None), P("band", None)),
        check_vma=False,
    )
```

```python
import functools

import jax
import jax.numpy as jnp
import ml_dtypes
import numpy as np
from jax import lax
from jax.experimental import pallas as pl
from jax.experimental.pallas import tpu as pltpu
from jax.sharding import PartitionSpec as P

CHUNKS = (32, 32)
LAYER = 8
LANES = 128
SUBLANES = 8
f32, bf16 = jnp.float32, jnp.bfloat16
VMEM = pl.BlockSpec(memory_space=pltpu.VMEM)


def tables(g):
    index = np.arange(g)
    angle = 2.0 * np.pi / g * (np.outer(index, index) % g)
    cas = np.cos(angle) + np.sin(angle)
    hi = cas.astype(np.float32).astype(ml_dtypes.bfloat16)
    lo = (cas - hi.astype(np.float64)).astype(np.float32).astype(ml_dtypes.bfloat16)
    rows = np.concatenate([hi, hi, lo], axis=1)
    eye = np.eye(LANES // g, dtype=np.float32)
    wide_hi = np.kron(eye, hi.astype(np.float32)).astype(ml_dtypes.bfloat16)
    wide_lo = np.kron(eye, lo.astype(np.float32)).astype(ml_dtypes.bfloat16)
    lanes = np.block([[wide_hi, wide_lo], [wide_hi, np.zeros_like(wide_lo)]])
    return jnp.asarray(rows), jnp.asarray(lanes)


def split(value):
    hi = value.astype(bf16)
    lo = (value - hi.astype(f32)).astype(bf16)
    return hi, lo


def rows_pass(table, value):
    hi, lo = split(value)
    stacked = jnp.concatenate([hi, lo, hi], axis=0)
    return jnp.dot(table, stacked, preferred_element_type=f32)


def lanes_pass(value, table):
    hi, lo = split(value)
    both = jnp.concatenate([hi, lo], axis=1)
    result = jnp.dot(both, table, preferred_element_type=f32)
    return result[:, :LANES] + result[:, LANES:]


def exchange_halves(value, g):
    half = g // 2
    low = lax.broadcasted_iota(jnp.int32, (half, LANES), 1) < g
    parts = []
    for start in range(0, value.shape[0], g):
        first = value[start : start + half]
        second = value[start + half : start + g]
        parts.append(jnp.where(low, first, pltpu.roll(second, g, 1)))
        parts.append(jnp.where(low, pltpu.roll(first, g, 1), second))
    return jnp.concatenate(parts, axis=0)


def side_by_side(value, count):
    rows = value.shape[0] // count
    return jnp.concatenate([value[k * rows : (k + 1) * rows] for k in range(count)], axis=1)


def stacked(value):
    count = value.shape[1] // LANES
    return jnp.concatenate([value[:, k * LANES : (k + 1) * LANES] for k in range(count)], axis=0)


def pair_kernel(g, n_right, n_other, has_acc, tiles, *refs):
    refs = list(refs)
    left = refs.pop(0)
    parts = [refs.pop(0) for _ in range(n_right + n_other)]
    flag = refs.pop(0) if n_other else None
    acc, _ = (refs.pop(0), refs.pop(0)) if has_acc else (None, None)
    kern, rows_table, lanes_table, out, token, work, right, other, sems = refs
    half = g // 2
    count = g * g // LANES
    table = rows_table[...]
    wide = lanes_table[...]

    copies = []
    filled = 0
    for k, part in enumerate(parts):
        filled = 0 if k == n_right else filled
        place = pl.ds(filled, part.shape[0])
        whole = right if k < n_right else other
        copies.append(pltpu.make_async_copy(part, whole.at[place, :], sems.at[k]))
        filled += part.shape[0]
    for copy in copies:
        copy.start()
    for copy in copies:
        copy.wait()

    def right_block():
        if not parts:
            return left[...]
        if n_other:
            return jnp.where(flag[0] > 0, right[...], other[...])
        return right[...]

    value = stacked(rows_pass(table, left[...] * right_block()))
    work[...] = exchange_halves(lanes_pass(value, wide), g)

    value = jnp.concatenate([work[pl.ds(k, g, stride=half), :] for k in range(half)], axis=1)
    value = rows_pass(table, value) * side_by_side(kern[...], half)
    value = rows_pass(table, value)
    for k in range(half):
        work[pl.ds(k, g, stride=half), :] = value[:, k * LANES : (k + 1) * LANES]

    value = exchange_halves(lanes_pass(work[...], wide), g)
    value = rows_pass(table, side_by_side(value, count)) * right_block()
    if has_acc:
        value = acc[...] + value
    out[...] = stacked(value) if tiles else value
    token[...] = value[:SUBLANES, :LANES]


def pair(left, right, acc, kern, consts, other=(), flag=None, tiles=False):
    g = left.shape[0]
    points = g**3
    operands = [left, *right, *other]
    specs = [VMEM] + [pl.BlockSpec(memory_space=pl.ANY)] * (len(right) + len(other))
    if other:
        operands.append(flag)
        specs.append(pl.BlockSpec(memory_space=pltpu.SMEM))
    if acc is not None:
        operands += acc
        specs += [VMEM, pl.BlockSpec(memory_space=pl.ANY)]
    operands += [kern, *consts]
    specs += [VMEM] * 3
    shape = (points // LANES, LANES) if tiles else left.shape
    return pl.pallas_call(
        functools.partial(pair_kernel, g, len(right), len(other), acc is not None, tiles),
        out_shape=[
            jax.ShapeDtypeStruct(shape, f32),
            jax.ShapeDtypeStruct((SUBLANES, LANES), f32),
        ],
        in_specs=specs,
        out_specs=[VMEM] * 2,
        scratch_shapes=[
            pltpu.VMEM((points // LANES, LANES), f32),
            pltpu.VMEM(left.shape if right else (SUBLANES, LANES), f32),
            pltpu.VMEM(left.shape if other else (SUBLANES, LANES), f32),
            pltpu.SemaphoreType.DMA((max(1, len(right) + len(other)),)),
        ],
        compiler_params=pltpu.CompilerParams(vmem_limit_bytes=10 * 2**20),
        cost_estimate=pl.CostEstimate(flops=points, bytes_accessed=points, transcendentals=0),
    )(*operands)


def lookup_kernel(scale, values, index, out):
    g = index.shape[0]
    half = g // 2
    table = jnp.broadcast_to(values[...], (g, LANES))
    for step in range(g * g // LANES):
        cols = slice(step * LANES, (step + 1) * LANES)
        found = jnp.take_along_axis(table, index[:, cols], axis=1) * scale
        found = exchange_halves(found, g)
        for k in range(2):
            out[pl.ds(2 * step + k, half, stride=g), :] = found[k * half : (k + 1) * half]


def lookup(kernel_values, shell_index):
    g = shell_index.shape[0]
    classes = kernel_values.shape[0]
    padded = jnp.pad(kernel_values, (0, LANES - classes)).reshape(1, LANES)
    return pl.pallas_call(
        functools.partial(lookup_kernel, -1.0 / g**3),
        out_shape=jax.ShapeDtypeStruct((g**3 // LANES, LANES), f32),
        in_specs=[VMEM] * 2,
        out_specs=VMEM,
        compiler_params=pltpu.CompilerParams(vmem_limit_bytes=8 * 2**20),
    )(padded, shell_index)


def tile_kernel(own, tiles):
    tiles[...] = stacked(own[...])


def tiled(own):
    return pl.pallas_call(
        tile_kernel,
        out_shape=jax.ShapeDtypeStruct((own.size // LANES, LANES), f32),
        in_specs=[VMEM],
        out_specs=VMEM,
        compiler_params=pltpu.CompilerParams(vmem_limit_bytes=8 * 2**20),
    )(own)


def regroup_kernel(place, columns, done, *outs):
    rows = outs[0].shape[1]
    for k, out in enumerate(outs):
        first = pl.multiple_of(jnp.bitwise_xor(place[0], k) * rows, rows)
        out[...] = columns[:, pl.ds(first, rows), :]


def regroup(columns, place, done):
    layers, rows = columns.shape[0], columns.shape[1] // LAYER
    return pl.pallas_call(
        regroup_kernel,
        out_shape=[jax.ShapeDtypeStruct((layers, rows, LANES), f32)] * LAYER,
        in_specs=[pl.BlockSpec(memory_space=pltpu.SMEM), VMEM, pl.BlockSpec(memory_space=pl.ANY)],
        out_specs=[VMEM] * LAYER,
        compiler_params=pltpu.CompilerParams(vmem_limit_bytes=8 * 2**20),
    )(place, columns, done)


def margin_kernel(scale, place, terms, *refs):
    orbitals, out = refs[:-1], refs[-1]
    count = terms.shape[0]
    lefts, rights = [], []
    for step in range(terms.shape[1] // SUBLANES):
        rows = slice(step * SUBLANES, (step + 1) * SUBLANES)
        part = [column[k, rows, :] for k in range(count // LAYER) for column in orbitals]
        a_hi, a_lo = split(jnp.concatenate(part, axis=0))
        b_hi, b_lo = split(terms[:, rows, :].reshape(count * SUBLANES, LANES))
        lefts += [a_hi, a_lo, a_hi]
        rights += [b_hi, b_hi, b_lo]
    products = lax.dot_general(
        jnp.concatenate(lefts, axis=1),
        jnp.concatenate(rights, axis=1),
        (((1,), (1,)), ((), ())),
        preferred_element_type=f32,
    )
    size = count * SUBLANES
    row = lax.broadcasted_iota(jnp.int32, (size, size), 0) % SUBLANES
    col = lax.broadcasted_iota(jnp.int32, (size, size), 1) % SUBLANES
    kept = jnp.where(row == col, products, 0.0)
    summed = jnp.sum(kept.reshape(count, SUBLANES, size), axis=1)
    pick_row = lax.broadcasted_iota(jnp.int32, (size, count), 0) // SUBLANES
    pick_col = lax.broadcasted_iota(jnp.int32, (size, count), 1)
    pick = (pick_row == pick_col).astype(f32)
    highest = lax.Precision.HIGHEST
    by_distance = jnp.dot(summed, pick, precision=highest, preferred_element_type=f32)
    row = lax.broadcasted_iota(jnp.int32, (count, count), 0)
    col = lax.broadcasted_iota(jnp.int32, (count, count), 1)
    order = (jnp.bitwise_xor(row, place[0]) == col).astype(f32)
    out[...] = scale * jnp.dot(order, by_distance, precision=highest, preferred_element_type=f32)


def partial_margin(orbitals, terms, place, points):
    count = terms.shape[0]
    return pl.pallas_call(
        functools.partial(margin_kernel, 1.0 / points),
        out_shape=jax.ShapeDtypeStruct((count, count), f32),
        in_specs=[pl.BlockSpec(memory_space=pltpu.SMEM)] + [VMEM] * (1 + len(orbitals)),
        out_specs=VMEM,
        compiler_params=pltpu.CompilerParams(
            vmem_limit_bytes=8 * 2**20 + 12 * (count * SUBLANES) ** 2
        ),
    )(place, terms, *orbitals)


def permute(value, target, count):
    return lax.ppermute(value, "band", [(source, target(source) % count) for source in range(count)])


def far_target(source):
    return source - 4 if (source // 2) % 2 else source + 4


def after(*values):
    return lax.optimization_barrier(values)


def exchange(value, groups=None):
    return lax.all_to_all(
        value, "band", split_axis=0, concat_axis=0, tiled=True, axis_index_groups=groups
    )


def local(orbitals, kernel_values, shell_index):
    count = lax.axis_size("band")
    me = lax.axis_index("band")
    g = shell_index.shape[0]
    points = g**3
    consts = tables(g)
    own = orbitals.reshape(g, g * g)
    layers = count // LAYER
    along = [[layer * LAYER + k for layer in range(layers)] for k in range(LAYER)]

    def swap(value, distance=1):
        return permute(value, lambda d: d ^ distance, count)

    starts = [sum(CHUNKS[:k]) for k in range(len(CHUNKS))]
    near = [swap(own[start : start + size], 2) for start, size in zip(starts, CHUNKS)]
    peer = swap(own)
    by_tile, kernel_values = after(tiled(own), kernel_values)
    columns = exchange(by_tile.reshape(layers, -1, LANES), along)

    kern = lookup(kernel_values, shell_index)
    far = [None] * 2
    term, done = pair(own, [], None, kern, consts)
    near[0], done = after(near[0], done)
    far[0] = permute(near[0], far_target, count)
    term, done = pair(own, [peer], (term, done), kern, consts)
    near[1], done = after(near[1], done)
    far[1] = permute(near[1], far_target, count)
    near_cross = [swap(part) for part in near]
    use_near = (((me + 1) // 2) % 2).astype(jnp.int32).reshape(1)
    term, done = pair(own, near, (term, done), kern, consts)
    far[1], done = after(far[1], done)
    far_cross = [swap(part) for part in far]
    term, done = pair(own, far, (term, done), kern, consts)
    tiles, done = pair(own, near_cross, (term, done), kern, consts, far_cross, use_near, tiles=True)
    place = (me % LAYER).astype(jnp.int32).reshape(1)
    columns = list(regroup(columns, place, done))
    columns = [columns[0]] + [swap(columns[k], k) for k in range(1, LAYER)]
    spread_terms = exchange(tiles.reshape(count, -1, LANES))
    term = tiles.reshape(g * g // LANES, g, LANES).transpose(1, 0, 2).reshape(orbitals.shape)
    rows = partial_margin(columns, spread_terms, place, points)
    margin = jnp.sum(exchange(rows), axis=0, keepdims=True)
    return term, margin


def solution(mesh):
    return jax.shard_map(
        local,
        mesh=mesh,
        in_specs=(P("band", None, None), P(), P()),
        out_specs=(P("band", None, None), P("band", None)),
        check_vma=False,
    )
```

```python
import functools

import jax
import jax.numpy as jnp
import ml_dtypes
import numpy as np
from jax import lax
from jax.experimental import pallas as pl
from jax.experimental.pallas import tpu as pltpu
from jax.sharding import PartitionSpec as P

CHUNKS = (32, 32)
LAYER = 8
LANES = 128
SUBLANES = 8
f32, bf16 = jnp.float32, jnp.bfloat16
VMEM = pl.BlockSpec(memory_space=pltpu.VMEM)


def tables(g):
    index = np.arange(g)
    angle = 2.0 * np.pi / g * (np.outer(index, index) % g)
    cas = np.cos(angle) + np.sin(angle)
    hi = cas.astype(np.float32).astype(ml_dtypes.bfloat16)
    lo = (cas - hi.astype(np.float64)).astype(np.float32).astype(ml_dtypes.bfloat16)
    rows = np.concatenate([hi, hi, lo], axis=1)
    eye = np.eye(LANES // g, dtype=np.float32)
    wide_hi = np.kron(eye, hi.astype(np.float32)).astype(ml_dtypes.bfloat16)
    wide_lo = np.kron(eye, lo.astype(np.float32)).astype(ml_dtypes.bfloat16)
    lanes = np.block([[wide_hi, wide_lo], [wide_hi, np.zeros_like(wide_lo)]])
    return jnp.asarray(rows), jnp.asarray(lanes)


def split(value):
    hi = value.astype(bf16)
    lo = (value - hi.astype(f32)).astype(bf16)
    return hi, lo


def rows_pass(table, value):
    hi, lo = split(value)
    stacked = jnp.concatenate([hi, lo, hi], axis=0)
    return jnp.dot(table, stacked, preferred_element_type=f32)


def lanes_pass(value, table):
    hi, lo = split(value)
    both = jnp.concatenate([hi, lo], axis=1)
    result = jnp.dot(both, table, preferred_element_type=f32)
    return result[:, :LANES] + result[:, LANES:]


def exchange_halves(value, g):
    half = g // 2
    low = lax.broadcasted_iota(jnp.int32, (half, LANES), 1) < g
    parts = []
    for start in range(0, value.shape[0], g):
        first = value[start : start + half]
        second = value[start + half : start + g]
        parts.append(jnp.where(low, first, pltpu.roll(second, g, 1)))
        parts.append(jnp.where(low, pltpu.roll(first, g, 1), second))
    return jnp.concatenate(parts, axis=0)


def side_by_side(value, count):
    rows = value.shape[0] // count
    return jnp.concatenate([value[k * rows : (k + 1) * rows] for k in range(count)], axis=1)


def stacked(value):
    count = value.shape[1] // LANES
    return jnp.concatenate([value[:, k * LANES : (k + 1) * LANES] for k in range(count)], axis=0)


def pair_kernel(g, n_right, n_other, has_acc, tiles, *refs):
    refs = list(refs)
    left = refs.pop(0)
    parts = [refs.pop(0) for _ in range(n_right + n_other)]
    flag = refs.pop(0) if n_other else None
    acc, _ = (refs.pop(0), refs.pop(0)) if has_acc else (None, None)
    kern, rows_table, lanes_table, out, token, work, right, other, sems = refs
    half = g // 2
    count = g * g // LANES
    table = rows_table[...]
    wide = lanes_table[...]

    copies = []
    filled = 0
    for k, part in enumerate(parts):
        filled = 0 if k == n_right else filled
        place = pl.ds(filled, part.shape[0])
        whole = right if k < n_right else other
        copies.append(pltpu.make_async_copy(part, whole.at[place, :], sems.at[k]))
        filled += part.shape[0]
    for copy in copies:
        copy.start()
    for copy in copies:
        copy.wait()

    def right_block():
        if not parts:
            return left[...]
        if n_other:
            return jnp.where(flag[0] > 0, right[...], other[...])
        return right[...]

    value = stacked(rows_pass(table, left[...] * right_block()))
    work[...] = exchange_halves(lanes_pass(value, wide), g)

    value = jnp.concatenate([work[pl.ds(k, g, stride=half), :] for k in range(half)], axis=1)
    value = rows_pass(table, value) * side_by_side(kern[...], half)
    value = rows_pass(table, value)
    for k in range(half):
        work[pl.ds(k, g, stride=half), :] = value[:, k * LANES : (k + 1) * LANES]

    value = exchange_halves(lanes_pass(work[...], wide), g)
    value = rows_pass(table, side_by_side(value, count)) * right_block()
    if has_acc:
        value = acc[...] + value
    out[...] = stacked(value) if tiles else value
    token[...] = value[:SUBLANES, :LANES]


def pair(left, right, acc, kern, consts, other=(), flag=None, tiles=False):
    g = left.shape[0]
    points = g**3
    operands = [left, *right, *other]
    specs = [VMEM] + [pl.BlockSpec(memory_space=pl.ANY)] * (len(right) + len(other))
    if other:
        operands.append(flag)
        specs.append(pl.BlockSpec(memory_space=pltpu.SMEM))
    if acc is not None:
        operands += acc
        specs += [VMEM, pl.BlockSpec(memory_space=pl.ANY)]
    operands += [kern, *consts]
    specs += [VMEM] * 3
    shape = (points // LANES, LANES) if tiles else left.shape
    return pl.pallas_call(
        functools.partial(pair_kernel, g, len(right), len(other), acc is not None, tiles),
        out_shape=[
            jax.ShapeDtypeStruct(shape, f32),
            jax.ShapeDtypeStruct((SUBLANES, LANES), f32),
        ],
        in_specs=specs,
        out_specs=[VMEM] * 2,
        scratch_shapes=[
            pltpu.VMEM((points // LANES, LANES), f32),
            pltpu.VMEM(left.shape if right else (SUBLANES, LANES), f32),
            pltpu.VMEM(left.shape if other else (SUBLANES, LANES), f32),
            pltpu.SemaphoreType.DMA((max(1, len(right) + len(other)),)),
        ],
        compiler_params=pltpu.CompilerParams(vmem_limit_bytes=10 * 2**20),
        cost_estimate=pl.CostEstimate(flops=points, bytes_accessed=points, transcendentals=0),
    )(*operands)


def lookup_kernel(scale, values, index, out):
    g = index.shape[0]
    half = g // 2
    table = jnp.broadcast_to(values[...], (g, LANES))
    for step in range(g * g // LANES):
        cols = slice(step * LANES, (step + 1) * LANES)
        found = jnp.take_along_axis(table, index[:, cols], axis=1) * scale
        found = exchange_halves(found, g)
        for k in range(2):
            out[pl.ds(2 * step + k, half, stride=g), :] = found[k * half : (k + 1) * half]


def lookup(kernel_values, shell_index):
    g = shell_index.shape[0]
    classes = kernel_values.shape[0]
    padded = jnp.pad(kernel_values, (0, LANES - classes)).reshape(1, LANES)
    return pl.pallas_call(
        functools.partial(lookup_kernel, -1.0 / g**3),
        out_shape=jax.ShapeDtypeStruct((g**3 // LANES, LANES), f32),
        in_specs=[VMEM] * 2,
        out_specs=VMEM,
        compiler_params=pltpu.CompilerParams(vmem_limit_bytes=8 * 2**20),
    )(padded, shell_index)


def pieces_kernel(g, place, own, *outs):
    tiles = outs[0].shape[0] // g
    for k, out in enumerate(outs):
        first = jnp.bitwise_xor(place[0], k) * tiles
        for t in range(tiles):
            cols = pl.ds(pl.multiple_of((first + t) * LANES, LANES), LANES)
            out[t * g : (t + 1) * g, :] = own[:, cols]


def cut_by_layer(own, place, layers):
    g = own.shape[0]
    rows = own.size // LANES // layers
    return pl.pallas_call(
        functools.partial(pieces_kernel, g),
        out_shape=[jax.ShapeDtypeStruct((rows, LANES), f32)] * layers,
        in_specs=[pl.BlockSpec(memory_space=pltpu.SMEM), VMEM],
        out_specs=[VMEM] * layers,
        compiler_params=pltpu.CompilerParams(vmem_limit_bytes=8 * 2**20),
    )(place, own)


def regroup_kernel(place, done, *refs):
    outs = refs[-LAYER:]
    rows = outs[0].shape[1]
    for k, out in enumerate(outs):
        first = pl.multiple_of(jnp.bitwise_xor(place[1], k) * rows, rows)
        for layer, piece in enumerate(refs[:-LAYER]):
            out[layer] = piece[pl.ds(first, rows), :]


def regroup(pieces, place, done):
    rows = pieces[0].shape[0] // LAYER
    return pl.pallas_call(
        regroup_kernel,
        out_shape=[jax.ShapeDtypeStruct((len(pieces), rows, LANES), f32)] * LAYER,
        in_specs=[pl.BlockSpec(memory_space=pltpu.SMEM), pl.BlockSpec(memory_space=pl.ANY)]
        + [VMEM] * len(pieces),
        out_specs=[VMEM] * LAYER,
        compiler_params=pltpu.CompilerParams(vmem_limit_bytes=8 * 2**20),
    )(place, done, *pieces)


def margin_kernel(scale, place, terms, *refs):
    orbitals, out = refs[:-1], refs[-1]
    count = terms.shape[0]
    lefts, rights = [], []
    for step in range(terms.shape[1] // SUBLANES):
        rows = slice(step * SUBLANES, (step + 1) * SUBLANES)
        part = [column[k, rows, :] for k in range(count // LAYER) for column in orbitals]
        a_hi, a_lo = split(jnp.concatenate(part, axis=0))
        b_hi, b_lo = split(terms[:, rows, :].reshape(count * SUBLANES, LANES))
        lefts += [a_hi, a_lo, a_hi]
        rights += [b_hi, b_hi, b_lo]
    products = lax.dot_general(
        jnp.concatenate(lefts, axis=1),
        jnp.concatenate(rights, axis=1),
        (((1,), (1,)), ((), ())),
        preferred_element_type=f32,
    )
    size = count * SUBLANES
    row = lax.broadcasted_iota(jnp.int32, (size, size), 0) % SUBLANES
    col = lax.broadcasted_iota(jnp.int32, (size, size), 1) % SUBLANES
    kept = jnp.where(row == col, products, 0.0)
    summed = jnp.sum(kept.reshape(count, SUBLANES, size), axis=1)
    pick_row = lax.broadcasted_iota(jnp.int32, (size, count), 0) // SUBLANES
    pick_col = lax.broadcasted_iota(jnp.int32, (size, count), 1)
    pick = (pick_row == pick_col).astype(f32)
    highest = lax.Precision.HIGHEST
    by_distance = jnp.dot(summed, pick, precision=highest, preferred_element_type=f32)
    row = lax.broadcasted_iota(jnp.int32, (count, count), 0)
    col = lax.broadcasted_iota(jnp.int32, (count, count), 1)
    order = (jnp.bitwise_xor(row, place[2]) == col).astype(f32)
    out[...] = scale * jnp.dot(order, by_distance, precision=highest, preferred_element_type=f32)


def partial_margin(orbitals, terms, place, points):
    count = terms.shape[0]
    return pl.pallas_call(
        functools.partial(margin_kernel, 1.0 / points),
        out_shape=jax.ShapeDtypeStruct((count, count), f32),
        in_specs=[pl.BlockSpec(memory_space=pltpu.SMEM)] + [VMEM] * (1 + len(orbitals)),
        out_specs=VMEM,
        compiler_params=pltpu.CompilerParams(
            vmem_limit_bytes=8 * 2**20 + 12 * (count * SUBLANES) ** 2
        ),
    )(place, terms, *orbitals)


def permute(value, target, count):
    return lax.ppermute(value, "band", [(source, target(source) % count) for source in range(count)])


def far_target(source):
    return source - 4 if (source // 2) % 2 else source + 4


def after(*values):
    return lax.optimization_barrier(values)


def exchange(value, groups=None):
    return lax.all_to_all(
        value, "band", split_axis=0, concat_axis=0, tiled=True, axis_index_groups=groups
    )


def local(orbitals, kernel_values, shell_index):
    count = lax.axis_size("band")
    me = lax.axis_index("band")
    g = shell_index.shape[0]
    points = g**3
    consts = tables(g)
    own = orbitals.reshape(g, g * g)
    layers = count // LAYER
    place = jnp.stack([me // LAYER, me % LAYER, me]).astype(jnp.int32)

    def swap(value, distance=1):
        return permute(value, lambda d: d ^ distance, count)

    starts = [sum(CHUNKS[:k]) for k in range(len(CHUNKS))]
    near = [swap(own[start : start + size], 2) for start, size in zip(starts, CHUNKS)]
    peer = swap(own)
    pieces = list(cut_by_layer(own, place, layers))
    pieces[:-1] = [pieces[0]] + [swap(pieces[k], k * LAYER) for k in range(1, layers - 1)]

    kern = lookup(kernel_values, shell_index)
    far = [None] * 2
    term, done = pair(own, [], None, kern, consts)
    near[0], pieces[1:-1], done = after(near[0], pieces[1:-1], done)
    far[0] = permute(near[0], far_target, count)
    term, done = pair(own, [peer], (term, done), kern, consts)
    near[1], done = after(near[1], done)
    far[1] = permute(near[1], far_target, count)
    near_cross = [swap(part) for part in near]
    use_near = (((me + 1) // 2) % 2).astype(jnp.int32).reshape(1)
    term, done = pair(own, near, (term, done), kern, consts)
    far[1], pieces[-1], done = after(far[1], pieces[-1], done)
    pieces[-1] = swap(pieces[-1], (layers - 1) * LAYER)
    far_cross = [swap(part) for part in far]
    term, done = pair(own, far, (term, done), kern, consts)
    tiles, done = pair(own, near_cross, (term, done), kern, consts, far_cross, use_near, tiles=True)
    tiles, pieces[-1] = after(tiles, pieces[-1])
    columns = list(regroup(pieces, place, done))
    columns = [columns[0]] + [swap(columns[k], k) for k in range(1, LAYER)]
    spread_terms = exchange(tiles.reshape(count, -1, LANES))
    term = tiles.reshape(g * g // LANES, g, LANES).transpose(1, 0, 2).reshape(orbitals.shape)
    rows = partial_margin(columns, spread_terms, place, points)
    margin = jnp.sum(exchange(rows), axis=0, keepdims=True)
    return term, margin


def solution(mesh):
    return jax.shard_map(
        local,
        mesh=mesh,
        in_specs=(P("band", None, None), P(), P()),
        out_specs=(P("band", None, None), P("band", None)),
        check_vma=False,
    )
```

```python
import functools

import jax
import jax.numpy as jnp
import ml_dtypes
import numpy as np
from jax import lax
from jax.experimental import pallas as pl
from jax.experimental.pallas import tpu as pltpu
from jax.sharding import PartitionSpec as P

CHUNKS = (1, 1)
LAYER = 8
LANES = 128
SUBLANES = 8
f32, bf16 = jnp.float32, jnp.bfloat16
VMEM = pl.BlockSpec(memory_space=pltpu.VMEM)


def tables(g):
    index = np.arange(g)
    angle = 2.0 * np.pi / g * (np.outer(index, index) % g)
    cas = np.cos(angle) + np.sin(angle)
    hi = cas.astype(np.float32).astype(ml_dtypes.bfloat16)
    lo = (cas - hi.astype(np.float64)).astype(np.float32).astype(ml_dtypes.bfloat16)
    rows = np.concatenate([hi, hi, lo], axis=1)
    eye = np.eye(LANES // g, dtype=np.float32)
    wide_hi = np.kron(eye, hi.astype(np.float32)).astype(ml_dtypes.bfloat16)
    wide_lo = np.kron(eye, lo.astype(np.float32)).astype(ml_dtypes.bfloat16)
    lanes = np.block([[wide_hi, wide_lo], [wide_hi, np.zeros_like(wide_lo)]])
    return jnp.asarray(rows), jnp.asarray(lanes)


def split(value):
    hi = value.astype(bf16)
    lo = (value - hi.astype(f32)).astype(bf16)
    return hi, lo


def three(value):
    hi, lo = split(value)
    last = (value - hi.astype(f32) - lo.astype(f32)).astype(bf16)
    return [hi, lo, last]


def rows_pass(table, value):
    hi, lo = split(value)
    stacked = jnp.concatenate([hi, lo, hi], axis=0)
    return jnp.dot(table, stacked, preferred_element_type=f32)


def lanes_pass(value, table):
    hi, lo = split(value)
    both = jnp.concatenate([hi, lo], axis=1)
    result = jnp.dot(both, table, preferred_element_type=f32)
    return result[:, :LANES] + result[:, LANES:]


def exchange_halves(value, g):
    half = g // 2
    low = lax.broadcasted_iota(jnp.int32, (half, LANES), 1) < g
    parts = []
    for start in range(0, value.shape[0], g):
        first = value[start : start + half]
        second = value[start + half : start + g]
        parts.append(jnp.where(low, first, pltpu.roll(second, g, 1)))
        parts.append(jnp.where(low, pltpu.roll(first, g, 1), second))
    return jnp.concatenate(parts, axis=0)


def side_by_side(value, count):
    rows = value.shape[0] // count
    return jnp.concatenate([value[k * rows : (k + 1) * rows] for k in range(count)], axis=1)


def stacked(value):
    count = value.shape[1] // LANES
    return jnp.concatenate([value[:, k * LANES : (k + 1) * LANES] for k in range(count)], axis=0)


def pair_kernel(g, n_right, n_other, has_acc, tiles, *refs):
    refs = list(refs)
    left = refs.pop(0)
    parts = [refs.pop(0) for _ in range(n_right + n_other)]
    flag = refs.pop(0) if n_other else None
    acc, _ = (refs.pop(0), refs.pop(0)) if has_acc else (None, None)
    kern, rows_table, lanes_table, out, token, work, right, sems = refs
    half = g // 2
    count = g * g // LANES
    table = rows_table[...]
    wide = lanes_table[...]

    def fetch(chosen):
        copies = []
        filled = 0
        for k, part in enumerate(chosen):
            place = pl.ds(filled, part.shape[0])
            copies.append(pltpu.make_async_copy(part, right.at[place, :], sems.at[k]))
            filled += part.shape[0]
        for copy in copies:
            copy.start()
        for copy in copies:
            copy.wait()

    if n_other:
        pl.when(flag[0] > 0)(functools.partial(fetch, parts[:n_right]))
        pl.when(flag[0] <= 0)(functools.partial(fetch, parts[n_right:]))
    else:
        fetch(parts)

    def right_block():
        return right[...] if parts else left[...]

    value = stacked(rows_pass(table, left[...] * right_block()))
    work[...] = exchange_halves(lanes_pass(value, wide), g)

    value = jnp.concatenate([work[pl.ds(k, g, stride=half), :] for k in range(half)], axis=1)
    value = rows_pass(table, value) * side_by_side(kern[...], half)
    value = rows_pass(table, value)
    for k in range(half):
        work[pl.ds(k, g, stride=half), :] = value[:, k * LANES : (k + 1) * LANES]

    value = exchange_halves(lanes_pass(work[...], wide), g)
    value = rows_pass(table, side_by_side(value, count)) * right_block()
    if has_acc:
        value = acc[...] + value
    out[...] = stacked(value) if tiles else value
    token[...] = value[:SUBLANES, :LANES]


def pair(left, right, acc, kern, consts, other=(), flag=None, tiles=False):
    g = left.shape[0]
    points = g**3
    operands = [left, *right, *other]
    specs = [VMEM] + [pl.BlockSpec(memory_space=pl.ANY)] * (len(right) + len(other))
    if other:
        operands.append(flag)
        specs.append(pl.BlockSpec(memory_space=pltpu.SMEM))
    if acc is not None:
        operands += acc
        specs += [VMEM, pl.BlockSpec(memory_space=pl.ANY)]
    operands += [kern, *consts]
    specs += [VMEM] * 3
    shape = (points // LANES, LANES) if tiles else left.shape
    return pl.pallas_call(
        functools.partial(pair_kernel, g, len(right), len(other), acc is not None, tiles),
        out_shape=[
            jax.ShapeDtypeStruct(shape, f32),
            jax.ShapeDtypeStruct((SUBLANES, LANES), f32),
        ],
        in_specs=specs,
        out_specs=[VMEM] * 2,
        scratch_shapes=[
            pltpu.VMEM((points // LANES, LANES), f32),
            pltpu.VMEM(left.shape if right else (SUBLANES, LANES), f32),
            pltpu.SemaphoreType.DMA((max(1, len(right), len(other)),)),
        ],
        compiler_params=pltpu.CompilerParams(vmem_limit_bytes=10 * 2**20),
        cost_estimate=pl.CostEstimate(flops=points, bytes_accessed=points, transcendentals=0),
    )(*operands)


def lookup_kernel(scale, values, index, out):
    g = index.shape[0]
    half = g // 2
    table = jnp.broadcast_to(values[...], (g, LANES))
    for step in range(g * g // LANES):
        cols = slice(step * LANES, (step + 1) * LANES)
        found = jnp.take_along_axis(table, index[:, cols], axis=1) * scale
        found = exchange_halves(found, g)
        for k in range(2):
            out[pl.ds(2 * step + k, half, stride=g), :] = found[k * half : (k + 1) * half]


def lookup(kernel_values, shell_index):
    g = shell_index.shape[0]
    classes = kernel_values.shape[0]
    padded = jnp.pad(kernel_values, (0, LANES - classes)).reshape(1, LANES)
    return pl.pallas_call(
        functools.partial(lookup_kernel, -1.0 / g**3),
        out_shape=jax.ShapeDtypeStruct((g**3 // LANES, LANES), f32),
        in_specs=[VMEM] * 2,
        out_specs=VMEM,
        compiler_params=pltpu.CompilerParams(vmem_limit_bytes=8 * 2**20),
    )(padded, shell_index)


def pieces_kernel(place, own, *refs):
    parts, outs = refs[: len(CHUNKS)], refs[len(CHUNKS) :]
    g = own.shape[0]
    start = 0
    for part in parts:
        part[...] = own[start : start + part.shape[0], :]
        start += part.shape[0]
    tiles = outs[0].shape[0] // g
    for k, out in enumerate(outs):
        first = jnp.bitwise_xor(place[0], k) * tiles
        for t in range(tiles):
            cols = pl.ds(pl.multiple_of((first + t) * LANES, LANES), LANES)
            out[t * g : (t + 1) * g, :] = own[:, cols]


def cut(own, place, layers):
    g = own.shape[0]
    rows = own.size // LANES // layers
    shapes = [(g * size // sum(CHUNKS), own.shape[1]) for size in CHUNKS] + [(rows, LANES)] * layers
    outs = pl.pallas_call(
        pieces_kernel,
        out_shape=[jax.ShapeDtypeStruct(shape, f32) for shape in shapes],
        in_specs=[pl.BlockSpec(memory_space=pltpu.SMEM), VMEM],
        out_specs=[VMEM] * len(shapes),
        compiler_params=pltpu.CompilerParams(vmem_limit_bytes=8 * 2**20),
    )(place, own)
    return outs[: len(CHUNKS)], list(outs[len(CHUNKS) :])


def regroup_kernel(place, done, *refs):
    outs = refs[-LAYER:]
    rows = outs[0].shape[1]
    for k, out in enumerate(outs):
        first = pl.multiple_of(jnp.bitwise_xor(place[1], k) * rows, rows)
        for layer, piece in enumerate(refs[:-LAYER]):
            out[layer] = piece[pl.ds(first, rows), :]


def regroup(pieces, place, done):
    rows = pieces[0].shape[0] // LAYER
    return pl.pallas_call(
        regroup_kernel,
        out_shape=[jax.ShapeDtypeStruct((len(pieces), rows, LANES), f32)] * LAYER,
        in_specs=[pl.BlockSpec(memory_space=pltpu.SMEM), pl.BlockSpec(memory_space=pl.ANY)]
        + [VMEM] * len(pieces),
        out_specs=[VMEM] * LAYER,
        compiler_params=pltpu.CompilerParams(vmem_limit_bytes=8 * 2**20),
    )(place, done, *pieces)


def margin_kernel(scale, place, terms, *refs):
    orbitals, out = refs[:-1], refs[-1]
    count = terms.shape[0]
    lefts, rights = [], []
    for step in range(terms.shape[1] // SUBLANES):
        rows = slice(step * SUBLANES, (step + 1) * SUBLANES)
        part = [column[k, rows, :] for k in range(count // LAYER) for column in orbitals]
        a_hi, a_lo = split(jnp.concatenate(part, axis=0))
        b_hi, b_lo = split(terms[:, rows, :].reshape(count * SUBLANES, LANES))
        lefts += [a_hi, a_lo, a_hi]
        rights += [b_hi, b_hi, b_lo]
    products = lax.dot_general(
        jnp.concatenate(lefts, axis=1),
        jnp.concatenate(rights, axis=1),
        (((1,), (1,)), ((), ())),
        preferred_element_type=f32,
    )
    size = count * SUBLANES
    row = lax.broadcasted_iota(jnp.int32, (size, size), 0) % SUBLANES
    col = lax.broadcasted_iota(jnp.int32, (size, size), 1) % SUBLANES
    kept = jnp.where(row == col, products, 0.0)
    summed = jnp.sum(kept.reshape(count, SUBLANES, size), axis=1)
    pick_row = lax.broadcasted_iota(jnp.int32, (size, count), 0) // SUBLANES
    pick_col = lax.broadcasted_iota(jnp.int32, (size, count), 1)
    pick = (pick_row == pick_col).astype(f32).astype(bf16)
    by_distance = jnp.dot(
        jnp.concatenate(three(summed), axis=1),
        jnp.concatenate([pick] * 3, axis=0),
        preferred_element_type=f32,
    )
    row = lax.broadcasted_iota(jnp.int32, (count, count), 0)
    col = lax.broadcasted_iota(jnp.int32, (count, count), 1)
    order = (jnp.bitwise_xor(row, place[2]) == col).astype(f32).astype(bf16)
    out[...] = scale * jnp.dot(
        jnp.concatenate([order] * 3, axis=1),
        jnp.concatenate(three(by_distance), axis=0),
        preferred_element_type=f32,
    )


def partial_margin(orbitals, terms, place, points):
    count = terms.shape[0]
    return pl.pallas_call(
        functools.partial(margin_kernel, 1.0 / points),
        out_shape=jax.ShapeDtypeStruct((count, count), f32),
        in_specs=[pl.BlockSpec(memory_space=pltpu.SMEM)] + [VMEM] * (1 + len(orbitals)),
        out_specs=VMEM,
        compiler_params=pltpu.CompilerParams(
            vmem_limit_bytes=8 * 2**20 + 12 * (count * SUBLANES) ** 2
        ),
    )(place, terms, *orbitals)


def permute(value, target, count):
    return lax.ppermute(value, "band", [(source, target(source) % count) for source in range(count)])


def far_target(source):
    return source - 4 if (source // 2) % 2 else source + 4


def after(*values):
    return lax.optimization_barrier(values)


def exchange(value, groups=None):
    return lax.all_to_all(
        value, "band", split_axis=0, concat_axis=0, tiled=True, axis_index_groups=groups
    )


def local(orbitals, kernel_values, shell_index):
    count = lax.axis_size("band")
    me = lax.axis_index("band")
    g = shell_index.shape[0]
    points = g**3
    consts = tables(g)
    own = orbitals.reshape(g, g * g)
    layers = count // LAYER
    place = jnp.stack([me // LAYER, me % LAYER, me]).astype(jnp.int32)

    def swap(value, distance=1):
        return permute(value, lambda d: d ^ distance, count)

    parts, pieces = cut(own, place, layers)
    near = [swap(part, 2) for part in parts]
    peer = swap(own)
    pieces[:-1] = [pieces[0]] + [swap(pieces[k], k * LAYER) for k in range(1, layers - 1)]

    kern = lookup(kernel_values, shell_index)
    far = [None] * 2
    term, done = pair(own, [], None, kern, consts)
    near[0], pieces[1:-1], done = after(near[0], pieces[1:-1], done)
    far[0] = permute(near[0], far_target, count)
    term, done = pair(own, [peer], (term, done), kern, consts)
    near[1], done = after(near[1], done)
    far[1] = permute(near[1], far_target, count)
    near_cross = [swap(part) for part in near]
    use_near = (((me + 1) // 2) % 2).astype(jnp.int32).reshape(1)
    term, done = pair(own, near, (term, done), kern, consts)
    far[1], pieces[-1], done = after(far[1], pieces[-1], done)
    pieces[-1] = swap(pieces[-1], (layers - 1) * LAYER)
    far_cross = [swap(part) for part in far]
    term, done = pair(own, far, (term, done), kern, consts)
    tiles, done = pair(own, near_cross, (term, done), kern, consts, far_cross, use_near, tiles=True)
    tiles, pieces[-1] = after(tiles, pieces[-1])
    columns = list(regroup(pieces, place, done))
    columns = [columns[0]] + [swap(columns[k], k) for k in range(1, LAYER)]
    spread_terms = exchange(tiles.reshape(count, -1, LANES))
    term = tiles.reshape(g * g // LANES, g, LANES).transpose(1, 0, 2).reshape(orbitals.shape)
    rows = partial_margin(columns, spread_terms, place, points)
    margin = jnp.sum(exchange(rows), axis=0, keepdims=True)
    return term, margin


def solution(mesh):
    return jax.shard_map(
        local,
        mesh=mesh,
        in_specs=(P("band", None, None), P(), P()),
        out_specs=(P("band", None, None), P("band", None)),
        check_vma=False,
    )
```

```python
import functools

import jax
import jax.numpy as jnp
import ml_dtypes
import numpy as np
from jax import lax
from jax.experimental import pallas as pl
from jax.experimental.pallas import tpu as pltpu
from jax.sharding import PartitionSpec as P

CHUNKS = (1, 1)
LAYER = 8
LANES = 128
SUBLANES = 8
f32, bf16 = jnp.float32, jnp.bfloat16
VMEM = pl.BlockSpec(memory_space=pltpu.VMEM)


def tables(g):
    index = np.arange(g)
    angle = 2.0 * np.pi / g * (np.outer(index, index) % g)
    cas = np.cos(angle) + np.sin(angle)
    hi = cas.astype(np.float32).astype(ml_dtypes.bfloat16)
    lo = (cas - hi.astype(np.float64)).astype(np.float32).astype(ml_dtypes.bfloat16)
    rows = np.concatenate([hi, hi, lo], axis=1)
    eye = np.eye(LANES // g, dtype=np.float32)
    wide_hi = np.kron(eye, hi.astype(np.float32)).astype(ml_dtypes.bfloat16)
    wide_lo = np.kron(eye, lo.astype(np.float32)).astype(ml_dtypes.bfloat16)
    lanes = np.block([[wide_hi, wide_lo], [wide_hi, np.zeros_like(wide_lo)]])
    return jnp.asarray(rows), jnp.asarray(lanes)


def split(value):
    hi = value.astype(bf16)
    lo = (value - hi.astype(f32)).astype(bf16)
    return hi, lo


def three(value):
    hi, lo = split(value)
    last = (value - hi.astype(f32) - lo.astype(f32)).astype(bf16)
    return [hi, lo, last]


def rows_pass(table, value):
    hi, lo = split(value)
    stacked = jnp.concatenate([hi, lo, hi], axis=0)
    return jnp.dot(table, stacked, preferred_element_type=f32)


def lanes_pass(value, table):
    hi, lo = split(value)
    both = jnp.concatenate([hi, lo], axis=1)
    result = jnp.dot(both, table, preferred_element_type=f32)
    return result[:, :LANES] + result[:, LANES:]


def exchange_halves(value, g):
    half = g // 2
    low = lax.broadcasted_iota(jnp.int32, (half, LANES), 1) < g
    parts = []
    for start in range(0, value.shape[0], g):
        first = value[start : start + half]
        second = value[start + half : start + g]
        parts.append(jnp.where(low, first, pltpu.roll(second, g, 1)))
        parts.append(jnp.where(low, pltpu.roll(first, g, 1), second))
    return jnp.concatenate(parts, axis=0)


def side_by_side(value, count):
    rows = value.shape[0] // count
    return jnp.concatenate([value[k * rows : (k + 1) * rows] for k in range(count)], axis=1)


def stacked(value):
    count = value.shape[1] // LANES
    return jnp.concatenate([value[:, k * LANES : (k + 1) * LANES] for k in range(count)], axis=0)


def pair_kernel(g, n_right, n_other, has_acc, tiles, *refs):
    refs = list(refs)
    left = refs.pop(0)
    parts = [refs.pop(0) for _ in range(n_right + n_other)]
    flag = refs.pop(0) if n_other else None
    acc, _ = (refs.pop(0), refs.pop(0)) if has_acc else (None, None)
    kern, rows_table, lanes_table, out, token, work, right, sems = refs
    half = g // 2
    count = g * g // LANES
    table = rows_table[...]
    wide = lanes_table[...]

    def fetch(chosen):
        copies = []
        filled = 0
        for k, part in enumerate(chosen):
            place = pl.ds(filled, part.shape[0])
            copies.append(pltpu.make_async_copy(part, right.at[place, :], sems.at[k]))
            filled += part.shape[0]
        for copy in copies:
            copy.start()
        for copy in copies:
            copy.wait()

    if n_other:
        pl.when(flag[0] > 0)(functools.partial(fetch, parts[:n_right]))
        pl.when(flag[0] <= 0)(functools.partial(fetch, parts[n_right:]))
    else:
        fetch(parts)

    def right_block():
        return right[...] if parts else left[...]

    value = stacked(rows_pass(table, left[...] * right_block()))
    work[...] = exchange_halves(lanes_pass(value, wide), g)

    value = jnp.concatenate([work[pl.ds(k, g, stride=half), :] for k in range(half)], axis=1)
    value = rows_pass(table, value) * side_by_side(kern[...], half)
    value = rows_pass(table, value)
    for k in range(half):
        work[pl.ds(k, g, stride=half), :] = value[:, k * LANES : (k + 1) * LANES]

    value = exchange_halves(lanes_pass(work[...], wide), g)
    value = rows_pass(table, side_by_side(value, count)) * right_block()
    if has_acc:
        value = acc[...] + value
    out[...] = stacked(value) if tiles else value
    token[...] = value[:SUBLANES, :LANES]


def pair(left, right, acc, kern, consts, other=(), flag=None, tiles=False):
    g = left.shape[0]
    points = g**3
    operands = [left, *right, *other]
    specs = [VMEM] + [pl.BlockSpec(memory_space=pl.ANY)] * (len(right) + len(other))
    if other:
        operands.append(flag)
        specs.append(pl.BlockSpec(memory_space=pltpu.SMEM))
    if acc is not None:
        operands += acc
        specs += [VMEM, pl.BlockSpec(memory_space=pl.ANY)]
    operands += [kern, *consts]
    specs += [VMEM] * 3
    shape = (points // LANES, LANES) if tiles else left.shape
    return pl.pallas_call(
        functools.partial(pair_kernel, g, len(right), len(other), acc is not None, tiles),
        out_shape=[
            jax.ShapeDtypeStruct(shape, f32),
            jax.ShapeDtypeStruct((SUBLANES, LANES), f32),
        ],
        in_specs=specs,
        out_specs=[VMEM] * 2,
        scratch_shapes=[
            pltpu.VMEM((points // LANES, LANES), f32),
            pltpu.VMEM(left.shape if right else (SUBLANES, LANES), f32),
            pltpu.SemaphoreType.DMA((max(1, len(right), len(other)),)),
        ],
        compiler_params=pltpu.CompilerParams(vmem_limit_bytes=10 * 2**20),
        cost_estimate=pl.CostEstimate(flops=points, bytes_accessed=points, transcendentals=0),
    )(*operands)


def lookup_kernel(scale, values, index, out):
    g = index.shape[0]
    half = g // 2
    table = jnp.broadcast_to(values[...], (g, LANES))
    for step in range(g * g // LANES):
        cols = slice(step * LANES, (step + 1) * LANES)
        found = jnp.take_along_axis(table, index[:, cols], axis=1) * scale
        found = exchange_halves(found, g)
        for k in range(2):
            out[pl.ds(2 * step + k, half, stride=g), :] = found[k * half : (k + 1) * half]


def lookup(kernel_values, shell_index):
    g = shell_index.shape[0]
    classes = kernel_values.shape[0]
    padded = jnp.pad(kernel_values, (0, LANES - classes)).reshape(1, LANES)
    return pl.pallas_call(
        functools.partial(lookup_kernel, -1.0 / g**3),
        out_shape=jax.ShapeDtypeStruct((g**3 // LANES, LANES), f32),
        in_specs=[VMEM] * 2,
        out_specs=VMEM,
        compiler_params=pltpu.CompilerParams(vmem_limit_bytes=8 * 2**20),
    )(padded, shell_index)


def pieces_kernel(place, own, *refs):
    parts, outs = refs[: len(CHUNKS)], refs[len(CHUNKS) :]
    g = own.shape[0]
    start = 0
    for part in parts:
        part[...] = own[start : start + part.shape[0], :]
        start += part.shape[0]
    tiles = outs[0].shape[0] // g
    for k, out in enumerate(outs):
        first = jnp.bitwise_xor(place[0], k + 1) * tiles
        for t in range(tiles):
            cols = pl.ds(pl.multiple_of((first + t) * LANES, LANES), LANES)
            out[t * g : (t + 1) * g, :] = own[:, cols]


def cut(own, place, layers):
    g = own.shape[0]
    rows = own.size // LANES // layers
    shapes = [(g * size // sum(CHUNKS), own.shape[1]) for size in CHUNKS]
    shapes += [(rows, LANES)] * (layers - 1)
    outs = pl.pallas_call(
        pieces_kernel,
        out_shape=[jax.ShapeDtypeStruct(shape, f32) for shape in shapes],
        in_specs=[pl.BlockSpec(memory_space=pltpu.SMEM), VMEM],
        out_specs=[VMEM] * len(shapes),
        compiler_params=pltpu.CompilerParams(vmem_limit_bytes=8 * 2**20),
    )(place, own)
    return outs[: len(CHUNKS)], list(outs[len(CHUNKS) :])


def regroup_kernel(place, done, own, *refs):
    outs, pieces = refs[-LAYER:], refs[:-LAYER]
    g = own.shape[0]
    rows = outs[0].shape[1]
    for k, out in enumerate(outs):
        first = pl.multiple_of(jnp.bitwise_xor(place[1], k) * rows, rows)
        start = place[0] * (LAYER * rows) + first
        tile = pl.ds(pl.multiple_of(start // g * LANES, LANES), LANES)
        out[0] = own[pl.ds(pl.multiple_of(start % g, rows), rows), tile]
        for n, piece in enumerate(pieces):
            out[n + 1] = piece[pl.ds(first, rows), :]


def regroup(own, pieces, place, done):
    rows = pieces[0].shape[0] // LAYER
    return pl.pallas_call(
        regroup_kernel,
        out_shape=[jax.ShapeDtypeStruct((1 + len(pieces), rows, LANES), f32)] * LAYER,
        in_specs=[pl.BlockSpec(memory_space=pltpu.SMEM), pl.BlockSpec(memory_space=pl.ANY)]
        + [VMEM] * (1 + len(pieces)),
        out_specs=[VMEM] * LAYER,
        compiler_params=pltpu.CompilerParams(vmem_limit_bytes=8 * 2**20),
    )(place, done, own, *pieces)


def margin_kernel(scale, place, terms, *refs):
    orbitals, out = refs[:-1], refs[-1]
    count = terms.shape[0]
    lefts, rights = [], []
    for step in range(terms.shape[1] // SUBLANES):
        rows = slice(step * SUBLANES, (step + 1) * SUBLANES)
        part = [column[k, rows, :] for k in range(count // LAYER) for column in orbitals]
        a_hi, a_lo = split(jnp.concatenate(part, axis=0))
        b_hi, b_lo = split(terms[:, rows, :].reshape(count * SUBLANES, LANES))
        lefts += [a_hi, a_lo, a_hi]
        rights += [b_hi, b_hi, b_lo]
    products = lax.dot_general(
        jnp.concatenate(lefts, axis=1),
        jnp.concatenate(rights, axis=1),
        (((1,), (1,)), ((), ())),
        preferred_element_type=f32,
    )
    size = count * SUBLANES
    row = lax.broadcasted_iota(jnp.int32, (size, size), 0) % SUBLANES
    col = lax.broadcasted_iota(jnp.int32, (size, size), 1) % SUBLANES
    kept = jnp.where(row == col, products, 0.0)
    summed = jnp.sum(kept.reshape(count, SUBLANES, size), axis=1)
    pick_row = lax.broadcasted_iota(jnp.int32, (size, count), 0) // SUBLANES
    pick_col = lax.broadcasted_iota(jnp.int32, (size, count), 1)
    pick = (pick_row == pick_col).astype(f32).astype(bf16)
    by_distance = jnp.dot(
        jnp.concatenate(three(summed), axis=1),
        jnp.concatenate([pick] * 3, axis=0),
        preferred_element_type=f32,
    )
    row = lax.broadcasted_iota(jnp.int32, (count, count), 0)
    col = lax.broadcasted_iota(jnp.int32, (count, count), 1)
    order = (jnp.bitwise_xor(row, place[2]) == col).astype(f32).astype(bf16)
    out[...] = scale * jnp.dot(
        jnp.concatenate([order] * 3, axis=1),
        jnp.concatenate(three(by_distance), axis=0),
        preferred_element_type=f32,
    )


def partial_margin(orbitals, terms, place, points):
    count = terms.shape[0]
    return pl.pallas_call(
        functools.partial(margin_kernel, 1.0 / points),
        out_shape=jax.ShapeDtypeStruct((count, count), f32),
        in_specs=[pl.BlockSpec(memory_space=pltpu.SMEM)] + [VMEM] * (1 + len(orbitals)),
        out_specs=VMEM,
        compiler_params=pltpu.CompilerParams(
            vmem_limit_bytes=8 * 2**20 + 12 * (count * SUBLANES) ** 2
        ),
    )(place, terms, *orbitals)


def permute(value, target, count):
    return lax.ppermute(value, "band", [(source, target(source) % count) for source in range(count)])


def far_target(source):
    return source - 4 if (source // 2) % 2 else source + 4


def after(*values):
    return lax.optimization_barrier(values)


def exchange(value, groups=None):
    return lax.all_to_all(
        value, "band", split_axis=0, concat_axis=0, tiled=True, axis_index_groups=groups
    )


def local(orbitals, kernel_values, shell_index):
    count = lax.axis_size("band")
    me = lax.axis_index("band")
    g = shell_index.shape[0]
    points = g**3
    consts = tables(g)
    own = orbitals.reshape(g, g * g)
    layers = count // LAYER
    place = jnp.stack([me // LAYER, me % LAYER, me]).astype(jnp.int32)

    def swap(value, distance=1):
        return permute(value, lambda d: d ^ distance, count)

    parts, pieces = cut(own, place, layers)
    near = [swap(part, 2) for part in parts]
    peer = swap(own)
    pieces[:-1] = [swap(piece, (k + 1) * LAYER) for k, piece in enumerate(pieces[:-1])]

    kern = lookup(kernel_values, shell_index)
    far = [None] * 2
    term, done = pair(own, [], None, kern, consts)
    half = layers // 2 - 1
    near[0], pieces[:half], done = after(near[0], pieces[:half], done)
    far[0] = permute(near[0], far_target, count)
    term, done = pair(own, [peer], (term, done), kern, consts)
    near[1], pieces[half:-1], done = after(near[1], pieces[half:-1], done)
    far[1] = permute(near[1], far_target, count)
    near_cross = [swap(part) for part in near]
    use_near = (((me + 1) // 2) % 2).astype(jnp.int32).reshape(1)
    term, done = pair(own, near, (term, done), kern, consts)
    far[1], pieces[-1], done = after(far[1], pieces[-1], done)
    pieces[-1] = swap(pieces[-1], (layers - 1) * LAYER)
    far_cross = [swap(part) for part in far]
    term, done = pair(own, far, (term, done), kern, consts)
    tiles, done = pair(own, near_cross, (term, done), kern, consts, far_cross, use_near, tiles=True)
    tiles, pieces[-1] = after(tiles, pieces[-1])
    columns = list(regroup(own, pieces, place, done))
    columns = [columns[0]] + [swap(columns[k], k) for k in range(1, LAYER)]
    spread_terms = exchange(tiles.reshape(count, -1, LANES))
    term = tiles.reshape(g * g // LANES, g, LANES).transpose(1, 0, 2).reshape(orbitals.shape)
    rows = partial_margin(columns, spread_terms, place, points)
    margin = jnp.sum(exchange(rows), axis=0, keepdims=True)
    return term, margin


def solution(mesh):
    return jax.shard_map(
        local,
        mesh=mesh,
        in_specs=(P("band", None, None), P(), P()),
        out_specs=(P("band", None, None), P("band", None)),
        check_vma=False,
    )
```

```python
import functools

import jax
import jax.numpy as jnp
import ml_dtypes
import numpy as np
from jax import lax
from jax.experimental import pallas as pl
from jax.experimental.pallas import tpu as pltpu
from jax.sharding import PartitionSpec as P

CHUNKS = (1, 1)
LAYER = 8
LANES = 128
SUBLANES = 8
f32, bf16 = jnp.float32, jnp.bfloat16
VMEM = pl.BlockSpec(memory_space=pltpu.VMEM)


def tables(g):
    index = np.arange(g)
    angle = 2.0 * np.pi / g * (np.outer(index, index) % g)
    cas = np.cos(angle) + np.sin(angle)
    hi = cas.astype(np.float32).astype(ml_dtypes.bfloat16)
    lo = (cas - hi.astype(np.float64)).astype(np.float32).astype(ml_dtypes.bfloat16)
    rows = np.concatenate([hi, hi, lo], axis=1)
    eye = np.eye(LANES // g, dtype=np.float32)
    wide_hi = np.kron(eye, hi.astype(np.float32)).astype(ml_dtypes.bfloat16)
    wide_lo = np.kron(eye, lo.astype(np.float32)).astype(ml_dtypes.bfloat16)
    lanes = np.block([[wide_hi, wide_lo], [wide_hi, np.zeros_like(wide_lo)]])
    return jnp.asarray(rows), jnp.asarray(lanes)


def split(value):
    hi = value.astype(bf16)
    lo = (value - hi.astype(f32)).astype(bf16)
    return hi, lo


def three(value):
    hi, lo = split(value)
    last = (value - hi.astype(f32) - lo.astype(f32)).astype(bf16)
    return [hi, lo, last]


def rows_pass(table, value):
    hi, lo = split(value)
    stacked = jnp.concatenate([hi, lo, hi], axis=0)
    return jnp.dot(table, stacked, preferred_element_type=f32)


def lanes_pass(value, table):
    hi, lo = split(value)
    both = jnp.concatenate([hi, lo], axis=1)
    result = jnp.dot(both, table, preferred_element_type=f32)
    return result[:, :LANES] + result[:, LANES:]


def exchange_halves(value, g):
    half = g // 2
    low = lax.broadcasted_iota(jnp.int32, (half, LANES), 1) < g
    parts = []
    for start in range(0, value.shape[0], g):
        first = value[start : start + half]
        second = value[start + half : start + g]
        parts.append(jnp.where(low, first, pltpu.roll(second, g, 1)))
        parts.append(jnp.where(low, pltpu.roll(first, g, 1), second))
    return jnp.concatenate(parts, axis=0)


def side_by_side(value, count):
    rows = value.shape[0] // count
    return jnp.concatenate([value[k * rows : (k + 1) * rows] for k in range(count)], axis=1)


def stacked(value):
    count = value.shape[1] // LANES
    return jnp.concatenate([value[:, k * LANES : (k + 1) * LANES] for k in range(count)], axis=0)


def pair_kernel(g, n_right, n_other, has_acc, tiles, *refs):
    refs = list(refs)
    left = refs.pop(0)
    parts = [refs.pop(0) for _ in range(n_right + n_other)]
    flag = refs.pop(0) if n_other else None
    acc, _ = (refs.pop(0), refs.pop(0)) if has_acc else (None, None)
    kern, rows_table, lanes_table, out, token, work, right, sems = refs
    half = g // 2
    count = g * g // LANES
    table = rows_table[...]
    wide = lanes_table[...]

    def fetch(chosen):
        copies = []
        filled = 0
        for k, part in enumerate(chosen):
            place = pl.ds(filled, part.shape[0])
            copies.append(pltpu.make_async_copy(part, right.at[place, :], sems.at[k]))
            filled += part.shape[0]
        for copy in copies:
            copy.start()
        for copy in copies:
            copy.wait()

    if n_other:
        pl.when(flag[0] > 0)(functools.partial(fetch, parts[:n_right]))
        pl.when(flag[0] <= 0)(functools.partial(fetch, parts[n_right:]))
    else:
        fetch(parts)

    def right_block():
        return right[...] if parts else left[...]

    value = stacked(rows_pass(table, left[...] * right_block()))
    work[...] = exchange_halves(lanes_pass(value, wide), g)

    value = jnp.concatenate([work[pl.ds(k, g, stride=half), :] for k in range(half)], axis=1)
    value = rows_pass(table, value) * side_by_side(kern[...], half)
    value = rows_pass(table, value)
    for k in range(half):
        work[pl.ds(k, g, stride=half), :] = value[:, k * LANES : (k + 1) * LANES]

    value = exchange_halves(lanes_pass(work[...], wide), g)
    value = rows_pass(table, side_by_side(value, count)) * right_block()
    if has_acc:
        value = acc[...] + value
    out[...] = stacked(value) if tiles else value
    token[...] = value[:SUBLANES, :LANES]


def pair(left, right, acc, kern, consts, other=(), flag=None, tiles=False):
    g = left.shape[0]
    points = g**3
    operands = [left, *right, *other]
    specs = [VMEM] + [pl.BlockSpec(memory_space=pl.ANY)] * (len(right) + len(other))
    if other:
        operands.append(flag)
        specs.append(pl.BlockSpec(memory_space=pltpu.SMEM))
    if acc is not None:
        operands += acc
        specs += [VMEM, pl.BlockSpec(memory_space=pl.ANY)]
    operands += [kern, *consts]
    specs += [VMEM] * 3
    shape = (points // LANES, LANES) if tiles else left.shape
    return pl.pallas_call(
        functools.partial(pair_kernel, g, len(right), len(other), acc is not None, tiles),
        out_shape=[
            jax.ShapeDtypeStruct(shape, f32),
            jax.ShapeDtypeStruct((SUBLANES, LANES), f32),
        ],
        in_specs=specs,
        out_specs=[VMEM] * 2,
        scratch_shapes=[
            pltpu.VMEM((points // LANES, LANES), f32),
            pltpu.VMEM(left.shape if right else (SUBLANES, LANES), f32),
            pltpu.SemaphoreType.DMA((max(1, len(right), len(other)),)),
        ],
        compiler_params=pltpu.CompilerParams(vmem_limit_bytes=10 * 2**20),
        cost_estimate=pl.CostEstimate(flops=points, bytes_accessed=points, transcendentals=0),
    )(*operands)


def lookup_kernel(scale, values, index, out):
    g = index.shape[0]
    half = g // 2
    table = jnp.broadcast_to(values[...], (g, LANES))
    for step in range(g * g // LANES):
        cols = slice(step * LANES, (step + 1) * LANES)
        found = jnp.take_along_axis(table, index[:, cols], axis=1) * scale
        found = exchange_halves(found, g)
        for k in range(2):
            out[pl.ds(2 * step + k, half, stride=g), :] = found[k * half : (k + 1) * half]


def lookup(kernel_values, shell_index):
    g = shell_index.shape[0]
    classes = kernel_values.shape[0]
    padded = jnp.pad(kernel_values, (0, LANES - classes)).reshape(1, LANES)
    return pl.pallas_call(
        functools.partial(lookup_kernel, -1.0 / g**3),
        out_shape=jax.ShapeDtypeStruct((g**3 // LANES, LANES), f32),
        in_specs=[VMEM] * 2,
        out_specs=VMEM,
        compiler_params=pltpu.CompilerParams(vmem_limit_bytes=8 * 2**20),
    )(padded, shell_index)


def pieces_kernel(place, own, *refs):
    parts, outs, sems = refs[: len(CHUNKS)], refs[len(CHUNKS) : -1], refs[-1]
    g = own.shape[0]
    moves = []
    start = 0
    for part in parts:
        moves.append((own.at[pl.ds(start, part.shape[0]), :], part))
        start += part.shape[0]
    tiles = outs[0].shape[0] // g
    for k, out in enumerate(outs):
        first = jnp.bitwise_xor(place[0], k + 1) * tiles
        for t in range(tiles):
            cols = pl.ds(pl.multiple_of((first + t) * LANES, LANES), LANES)
            moves.append((own.at[:, cols], out.at[pl.ds(t * g, g), :]))
    copies = [
        pltpu.make_async_copy(source, target, sems.at[n])
        for n, (source, target) in enumerate(moves)
    ]
    for copy in copies:
        copy.start()
    for copy in copies:
        copy.wait()


def cut(own, place, layers):
    g = own.shape[0]
    rows = own.size // LANES // layers
    shapes = [(g * size // sum(CHUNKS), own.shape[1]) for size in CHUNKS]
    shapes += [(rows, LANES)] * (layers - 1)
    outs = pl.pallas_call(
        pieces_kernel,
        out_shape=[jax.ShapeDtypeStruct(shape, f32) for shape in shapes],
        in_specs=[
            pl.BlockSpec(memory_space=pltpu.SMEM),
            pl.BlockSpec(memory_space=pltpu.HBM),
        ],
        out_specs=[VMEM] * len(shapes),
        scratch_shapes=[
            pltpu.SemaphoreType.DMA((len(CHUNKS) + (layers - 1) * (rows // g),))
        ],
        compiler_params=pltpu.CompilerParams(vmem_limit_bytes=8 * 2**20),
    )(place, own)
    return outs[: len(CHUNKS)], list(outs[len(CHUNKS) :])


def regroup_kernel(place, done, own, *refs):
    outs, pieces = refs[-LAYER:], refs[:-LAYER]
    g = own.shape[0]
    rows = outs[0].shape[1]
    for k, out in enumerate(outs):
        first = pl.multiple_of(jnp.bitwise_xor(place[1], k) * rows, rows)
        start = place[0] * (LAYER * rows) + first
        tile = pl.ds(pl.multiple_of(start // g * LANES, LANES), LANES)
        out[0] = own[pl.ds(pl.multiple_of(start % g, rows), rows), tile]
        for n, piece in enumerate(pieces):
            out[n + 1] = piece[pl.ds(first, rows), :]


def regroup(own, pieces, place, done):
    rows = pieces[0].shape[0] // LAYER
    return pl.pallas_call(
        regroup_kernel,
        out_shape=[jax.ShapeDtypeStruct((1 + len(pieces), rows, LANES), f32)] * LAYER,
        in_specs=[pl.BlockSpec(memory_space=pltpu.SMEM), pl.BlockSpec(memory_space=pl.ANY)]
        + [VMEM] * (1 + len(pieces)),
        out_specs=[VMEM] * LAYER,
        compiler_params=pltpu.CompilerParams(vmem_limit_bytes=8 * 2**20),
    )(place, done, own, *pieces)


def margin_kernel(scale, place, terms, *refs):
    orbitals, out = refs[:-1], refs[-1]
    count = terms.shape[0]
    lefts, rights = [], []
    for step in range(terms.shape[1] // SUBLANES):
        rows = slice(step * SUBLANES, (step + 1) * SUBLANES)
        part = [column[k, rows, :] for k in range(count // LAYER) for column in orbitals]
        a_hi, a_lo = split(jnp.concatenate(part, axis=0))
        b_hi, b_lo = split(terms[:, rows, :].reshape(count * SUBLANES, LANES))
        lefts += [a_hi, a_lo, a_hi]
        rights += [b_hi, b_hi, b_lo]
    products = lax.dot_general(
        jnp.concatenate(lefts, axis=1),
        jnp.concatenate(rights, axis=1),
        (((1,), (1,)), ((), ())),
        preferred_element_type=f32,
    )
    size = count * SUBLANES
    row = lax.broadcasted_iota(jnp.int32, (size, size), 0) % SUBLANES
    col = lax.broadcasted_iota(jnp.int32, (size, size), 1) % SUBLANES
    kept = jnp.where(row == col, products, 0.0)
    summed = jnp.sum(kept.reshape(count, SUBLANES, size), axis=1)
    pick_row = lax.broadcasted_iota(jnp.int32, (size, count), 0) // SUBLANES
    pick_col = lax.broadcasted_iota(jnp.int32, (size, count), 1)
    pick = (pick_row == pick_col).astype(f32).astype(bf16)
    by_distance = jnp.dot(
        jnp.concatenate(three(summed), axis=1),
        jnp.concatenate([pick] * 3, axis=0),
        preferred_element_type=f32,
    )
    row = lax.broadcasted_iota(jnp.int32, (count, count), 0)
    col = lax.broadcasted_iota(jnp.int32, (count, count), 1)
    order = (jnp.bitwise_xor(row, place[2]) == col).astype(f32).astype(bf16)
    out[...] = scale * jnp.dot(
        jnp.concatenate([order] * 3, axis=1),
        jnp.concatenate(three(by_distance), axis=0),
        preferred_element_type=f32,
    )


def partial_margin(orbitals, terms, place, points):
    count = terms.shape[0]
    return pl.pallas_call(
        functools.partial(margin_kernel, 1.0 / points),
        out_shape=jax.ShapeDtypeStruct((count, count), f32),
        in_specs=[pl.BlockSpec(memory_space=pltpu.SMEM)] + [VMEM] * (1 + len(orbitals)),
        out_specs=VMEM,
        compiler_params=pltpu.CompilerParams(
            vmem_limit_bytes=8 * 2**20 + 12 * (count * SUBLANES) ** 2
        ),
    )(place, terms, *orbitals)


def permute(value, target, count):
    return lax.ppermute(value, "band", [(source, target(source) % count) for source in range(count)])


def far_target(source):
    return source - 4 if (source // 2) % 2 else source + 4


def after(*values):
    return lax.optimization_barrier(values)


def exchange(value, groups=None):
    return lax.all_to_all(
        value, "band", split_axis=0, concat_axis=0, tiled=True, axis_index_groups=groups
    )


def local(orbitals, kernel_values, shell_index):
    count = lax.axis_size("band")
    me = lax.axis_index("band")
    g = shell_index.shape[0]
    points = g**3
    consts = tables(g)
    own = orbitals.reshape(g, g * g)
    layers = count // LAYER
    place = jnp.stack([me // LAYER, me % LAYER, me]).astype(jnp.int32)

    def swap(value, distance=1):
        return permute(value, lambda d: d ^ distance, count)

    parts, pieces = cut(own, place, layers)
    near = [swap(part, 2) for part in parts]
    peer = swap(own)
    pieces[:-1] = [swap(piece, (k + 1) * LAYER) for k, piece in enumerate(pieces[:-1])]

    kern = lookup(kernel_values, shell_index)
    far = [None] * 2
    term, done = pair(own, [], None, kern, consts)
    half = layers // 2 - 1
    near[0], pieces[:half], done = after(near[0], pieces[:half], done)
    far[0] = permute(near[0], far_target, count)
    term, done = pair(own, [peer], (term, done), kern, consts)
    near[1], pieces[half:-1], done = after(near[1], pieces[half:-1], done)
    far[1] = permute(near[1], far_target, count)
    near_cross = [swap(part) for part in near]
    use_near = (((me + 1) // 2) % 2).astype(jnp.int32).reshape(1)
    term, done = pair(own, near, (term, done), kern, consts)
    far[1], pieces[-1], done = after(far[1], pieces[-1], done)
    pieces[-1] = swap(pieces[-1], (layers - 1) * LAYER)
    far_cross = [swap(part) for part in far]
    term, done = pair(own, far, (term, done), kern, consts)
    tiles, done = pair(own, near_cross, (term, done), kern, consts, far_cross, use_near, tiles=True)
    tiles, pieces[-1] = after(tiles, pieces[-1])
    columns = list(regroup(own, pieces, place, done))
    columns = [columns[0]] + [swap(columns[k], k) for k in range(1, LAYER)]
    spread_terms = exchange(tiles.reshape(count, -1, LANES))
    term = tiles.reshape(g * g // LANES, g, LANES).transpose(1, 0, 2).reshape(orbitals.shape)
    rows = partial_margin(columns, spread_terms, place, points)
    margin = jnp.sum(exchange(rows), axis=0, keepdims=True)
    return term, margin


def solution(mesh):
    return jax.shard_map(
        local,
        mesh=mesh,
        in_specs=(P("band", None, None), P(), P()),
        out_specs=(P("band", None, None), P("band", None)),
        check_vma=False,
    )
```
